512 devices in a mesh: grp: 16 (over y, core), shard: 32 (over x, z).
Axes of the slice: x: 4, y: 8, z: 8, core: 2. Of those that a mesh axis runs over, the one named last changes fastest.
Arguments:
- table: float32 [32768, 64], P('shard'), may hold values from -6 to 6
- accum: float32 [32768, 64], P('shard'), may hold values from 0.1 to 10
- grad_values: float32 [65536, 64], P(('grp', 'shard')), may hold values from -6 to 6
- grad_rows: int32 [65536], P(('grp', 'shard')), may hold values from 0 to 1023
- grad_counts: int32 [16384], P(('grp', 'shard')), may hold values from 1 to 4
- bucket_ids: int32 [131072, 24, 2], P(('grp', 'shard')), may hold values from 0 to 32767, as said below
- bag_lengths: int32 [131072, 24], P(('grp', 'shard')), may hold values from 1 to 2
- w_hidden: bfloat16 [1536, 1024], P('shard'), may hold values from -0.15625 to 0.15625
- b_hidden: float32 [1024], replicated, may hold values from -3 to 3
- w_score: bfloat16 [1024], replicated, may hold values from -0.1875 to 0.1875
Outputs:
- table_out: float32 [32768, 64], P('shard')
- accum_out: float32 [32768, 64], P('shard')
- scores: float32 [131072], P(('grp', 'shard'))
The draws below stay inside these ranges and needn't reach their ends.
Inputs may be any that keep to these rules, and one draw needn't show every extreme that they name: `bucket_ids`: counting all 24 x 2 id slots of a device's 256 requests, also those past a bag's length, and calling id // 1024 the owner: one owner gets exactly 768 of them, the same owner for every device of one group along grp, and every other owner's count differs from the others' by at most one.
All inputs are finite; a program needn't handle non-finite values.
Results may differ from the reference program's by a relative error of at most 0.0054.
Values may be sent and summed in bfloat16 or wider, within the bound.
No kernel may reach another device: no remote copies, remote signals or barrier semaphores. Data moves between devices by JAX's collectives and lax.ppermute only.
A program may use at most 64 MiB of HBM per device.

```python
import math
import jax
import jax.numpy as jnp
from jax import lax

E = 64
VOCABS = 24
HID = 1024
BAG = 2
ROWS_DEV = 1024
REQ_DEV = 256
ROWS = 32768
REQUESTS = 131072
GRADROWS = 65536
GSLOT = 4
CAP = 768
N_GRP = 16
N_SHARD = 32


def draw_bucket_ids(key, part):
    device_count = REQUESTS // REQ_DEV
    owner_count = ROWS // ROWS_DEV
    slot_count = REQ_DEV * VOCABS * BAG
    hot_key = jax.random.fold_in(key, 7)
    rest_key = jax.random.fold_in(key, 11)

    def one_device(device):
        group = device // owner_count
        hot_owner = jax.random.randint(jax.random.fold_in(hot_key, group), (), 0, owner_count)
        own_key = jax.random.fold_in(rest_key, device)
        perm_key, row_key = jax.random.split(own_key)
        index = jnp.arange(slot_count, dtype=jnp.int32)
        others = (hot_owner + 1 + (index - CAP) % (owner_count - 1)) % owner_count
        owners = jnp.where(index < CAP, hot_owner, others)
        owners = owners[jax.random.permutation(perm_key, slot_count)]
        row_ids = jax.random.randint(row_key, (slot_count,), 0, ROWS_DEV)
        return (owners * ROWS_DEV + row_ids).reshape(REQ_DEV, VOCABS, BAG)
    result = jax.vmap(one_device)(jnp.arange(device_count, dtype=jnp.int32))
    return result.reshape(REQUESTS, VOCABS, BAG).astype(jnp.int32)


def set_ends(drawn, key, low, largest):
    shape = drawn.shape
    spot = [jax.random.randint(jax.random.fold_in(key, axis), (), 0, shape[axis]) for axis in range(len(shape))]
    drawn = drawn.at[tuple(spot)].set(low)
    longest = shape.index(max(shape))
    spot[longest] = (spot[longest] + 1) % shape[longest]
    return drawn.at[tuple(spot)].set(largest)


def steps_of(key, dims, shards, least, top_value):
    def one(axis_at, parts):
        steps = jax.random.uniform(jax.random.fold_in(jax.random.fold_in(key, 6), axis_at), (parts,), jnp.float32, least / len(shards), top_value / len(shards))
        return jnp.repeat(jnp.exp(steps), dims[axis_at] // parts).reshape((-1,) + (1,) * (len(dims) - axis_at - 1))

    gain = one(*shards[0])
    for cut in shards[1:]:
        gain = gain * one(*cut)
    return gain


def bell_draw(rng, shape, scale, most, shards=(), kind=jnp.bfloat16):
    drawn = jax.random.normal(rng, shape, jnp.float32) * scale
    if len(shards) > 0:
        drawn = steps_of(rng, shape, shards, -0.22, 0.18) * drawn
    return jnp.clip(drawn, min=-most, max=most).astype(kind)


def setup_inputs(seed: int = 0) -> dict:
    streams_of = jax.random.split(jax.random.key(seed), 11)
    return {
        "table": bell_draw(streams_of[0], (ROWS, E), 1.0, 6.0, ((0, 32),), jnp.float32),
        "accum": jnp.clip(jnp.exp(math.log(10.0) - 4.6051702 * jax.random.uniform(streams_of[1], (ROWS, E), jnp.float32) ** steps_of(streams_of[1], (ROWS, E), ((0, 32),), -0.2, 0.2)), 0.1, 10.0),
        "grad_values": bell_draw(streams_of[2], (GRADROWS, E), 1.0, 6.0, ((0, 512),), jnp.float32),
        "grad_rows": set_ends(jax.random.randint(streams_of[3], (GRADROWS,), 0, ROWS_DEV), jax.random.fold_in(streams_of[3], 1), 0, ROWS_DEV - 1).astype(jnp.int32),
        "grad_counts": set_ends(jax.random.randint(streams_of[4], (N_GRP * N_SHARD * N_SHARD,), 1, GSLOT + 1), jax.random.fold_in(streams_of[4], 1), 1, GSLOT).astype(jnp.int32),
        "bucket_ids": draw_bucket_ids(jax.random.fold_in(streams_of[10], 71), 0),
        "bag_lengths": set_ends(jax.random.randint(streams_of[6], (REQUESTS, VOCABS), 1, BAG + 1), jax.random.fold_in(streams_of[6], 1), 1, BAG).astype(jnp.int32),
        "w_hidden": bell_draw(streams_of[7], (VOCABS * E, HID), (VOCABS * E) ** -0.5, 0.15625, ((0, 32),)),
        "b_hidden": bell_draw(streams_of[8], (HID,), 0.5, 3.0, (), jnp.float32),
        "w_score": bell_draw(streams_of[9], (HID,), HID ** -0.5, 0.1875),
    }


def reference(table, accum, grad_values, grad_rows, grad_counts, bucket_ids, bag_lengths, w_hidden, b_hidden, w_score):
    device_count = grad_counts.shape[0] // N_SHARD
    owner_ids = jnp.arange(N_SHARD, dtype=jnp.int32)
    targets = (owner_ids[None, :, None] * ROWS_DEV + grad_rows.reshape(device_count, N_SHARD, GSLOT)).reshape(-1)
    live_mask = jnp.arange(GSLOT, dtype=jnp.int32)[None, None, :] < grad_counts.reshape(device_count, N_SHARD)[:, :, None]
    slot_values = jnp.where(live_mask[..., None], grad_values.reshape(device_count, N_SHARD, GSLOT, E), 0.0).reshape(-1, E)
    grad_sum = jnp.zeros((ROWS, E), jnp.float32).at[targets].add(slot_values)
    accum_out = accum + grad_sum * grad_sum
    table_out = table - 0.5 * grad_sum * lax.rsqrt(accum_out)
    serving = table_out.astype(jnp.bfloat16)
    block_rows = math.gcd(REQUESTS, 4096)
    block_count = REQUESTS // block_rows

    def score_block(inputs):
        block_ids, block_lens = inputs
        gathered = serving[block_ids]
        in_bag = jnp.arange(BAG, dtype=jnp.int32)[None, None, :] < block_lens[:, :, None]
        pooled = lax.optimization_barrier(jnp.sum(jnp.where(in_bag[..., None], gathered.astype(jnp.float32), 0.0), axis=2))
        pooled = pooled.astype(jnp.bfloat16).reshape(block_rows, VOCABS * E)
        hidden_pre = jnp.dot(pooled, w_hidden, preferred_element_type=jnp.float32) + b_hidden
        hidden = jax.nn.silu(hidden_pre).astype(jnp.bfloat16)
        return jnp.dot(hidden, w_score, preferred_element_type=jnp.float32)
    scores = lax.map(score_block, (bucket_ids.reshape(block_count, block_rows, VOCABS, BAG), bag_lengths.reshape(block_count, block_rows, VOCABS)))
    return (table_out, accum_out, scores.reshape(REQUESTS))
```

```python
import functools

import jax
import jax.numpy as jnp
from jax import lax
from jax.experimental import pallas as pl
from jax.experimental.pallas import tpu as pltpu
from jax.sharding import Mesh
from jax.sharding import PartitionSpec as P

BF = jnp.bfloat16
F32 = jnp.float32
VMEM = pl.BlockSpec(memory_space=pltpu.VMEM)
SMEM = pl.BlockSpec(memory_space=pltpu.SMEM)
HALF = 8192
PARAMS = pltpu.CompilerParams(vmem_limit_bytes=56 * 2**20)


def message_kernel(values_t, rows, counts, out):
    owners, slots = counts.shape[1], rows.shape[1]
    per_owner = slots // owners
    spread = (
        lax.broadcasted_iota(jnp.int32, (owners, slots), 0)
        == lax.broadcasted_iota(jnp.int32, (owners, slots), 1) // per_owner
    ).astype(BF)
    many = jnp.broadcast_to(counts[...].astype(F32), (8, owners)).astype(BF)
    live = jnp.dot(many, spread, preferred_element_type=F32)
    place = lax.broadcasted_iota(jnp.int32, (1, slots), 1) % per_owner
    target = jnp.where(place < live[:1].astype(jnp.int32), rows[...], -64)
    high = jnp.broadcast_to(target >> 5, (64, slots)).astype(F32)
    low = jnp.broadcast_to(target & 31, (64, slots)).astype(F32)
    first = lax.broadcasted_iota(jnp.int32, (64, slots), 0) == 0
    digits = jnp.where(first, high, low)
    out[...] = jnp.concatenate([values_t[...], digits], axis=0).T.astype(BF)


def update_kernel(core, message, table_t, accum_t, table_out, accum_out, block):
    rows = table_t.shape[1]
    total = jnp.zeros((128, rows), F32)
    step = 512
    for start in range(0, message.shape[0], step):
        part = message[start : start + step]
        target = (part[:, 64:65].astype(F32) * 32.0 + part[:, 65:66].astype(F32)).astype(jnp.int32)
        picks = (target == lax.broadcasted_iota(jnp.int32, (step, rows), 1)).astype(F32).astype(BF)
        total += lax.dot_general(part, picks, (((0,), (0,)), ((), ())), preferred_element_type=F32)
    grad = total[:64]
    accum_new = accum_t[...] + grad * grad
    table_new = table_t[...] - 0.5 * grad * lax.rsqrt(accum_new)
    accum_out[...] = accum_new
    table_out[...] = table_new
    stacked = jnp.concatenate([table_new[:, : rows // 2], table_new[:, rows // 2 :]], axis=0)
    mine = jnp.where(core[0] == 0, stacked[:, : rows // 4], stacked[:, rows // 4 :])
    serving = mine.T.astype(BF)
    for i in range(block.shape[0]):
        block[i] = serving


def score_kernel(ids, own, other, weights, bias, head, out, rows, pooled):
    step = 256

    def spread(i, carry):
        start = pl.multiple_of(i * step, step)
        for k, half in enumerate((own, other)):
            value = half[pl.ds(start, step), :].astype(F32)
            rows[pl.ds(start + k * HALF, step), :] = value
            rows[pl.ds(start + (2 + k) * HALF, step), :] = pltpu.roll(value, 64, 1)
        return carry

    lax.fori_loop(0, HALF // step, spread, 0)
    rows[pl.ds(4 * HALF, 8), :] = jnp.zeros((8, 128), F32)
    left = lax.broadcasted_iota(jnp.int32, (1, 128), 1) < 64
    vocabs = ids.shape[0]

    def look_up(r, carry):
        for j in range(vocabs // 2):
            one = rows[pl.ds(ids[2 * j, 0, r], 1), :] + rows[pl.ds(ids[2 * j, 1, r], 1), :]
            two = rows[pl.ds(ids[2 * j + 1, 0, r], 1), :] + rows[pl.ds(ids[2 * j + 1, 1, r], 1), :]
            pooled[j, pl.ds(r, 1), :] = jnp.where(left, one, two)
        return carry

    lax.fori_loop(0, pooled.shape[1], look_up, 0)
    features = jnp.concatenate([pooled[j].astype(BF) for j in range(vocabs // 2)], axis=1)
    unit = jnp.dot(features, weights[...], preferred_element_type=F32) + bias[...]
    hidden = (unit / (1.0 + jnp.exp(-unit))).astype(BF)
    heads = jnp.broadcast_to(head[...].astype(F32), (8, head.shape[1])).astype(BF)
    out[...] = lax.dot_general(heads, hidden, (((1,), (1,)), ((), ())), preferred_element_type=F32)


def per_device(
    table,
    accum,
    grad_values,
    grad_rows,
    grad_counts,
    bucket_ids,
    bag_lengths,
    w_hidden,
    b_hidden,
    w_score,
):
    core = lax.axis_index("c")
    weights = lax.all_gather(w_hidden, ("x", "z"), axis=0, tiled=True)
    message = pl.pallas_call(
        message_kernel,
        out_shape=jax.ShapeDtypeStruct((128, 128), BF),
        in_specs=[VMEM] * 3,
        out_specs=VMEM,
        name="message",
    )(grad_values.T, grad_rows[None, :], grad_counts[None, :])
    got = lax.all_to_all(message.reshape(32, 4, 128), ("x", "z"), 0, 0, tiled=True)
    slots = lax.all_gather(got, ("y", "c"), axis=0, tiled=True).reshape(2048, 128)
    table_out, accum_out, block = pl.pallas_call(
        update_kernel,
        out_shape=(
            jax.ShapeDtypeStruct((64, 1024), F32),
            jax.ShapeDtypeStruct((64, 1024), F32),
            jax.ShapeDtypeStruct((8, 256, 128), BF),
        ),
        in_specs=[SMEM] + [VMEM] * 3,
        out_specs=(VMEM,) * 3,
        compiler_params=PARAMS,
        name="update",
    )(core[None], slots, table.T, accum.T)
    column = lax.all_to_all(block, "z", 0, 0, tiled=True).reshape(1, 2048, 128)
    own = lax.all_to_all(jnp.broadcast_to(column, (4, 2048, 128)), "x", 0, 0, tiled=True).reshape(HALF, 128)
    other = lax.ppermute(own, "c", [(0, 1), (1, 0)])

    ids = bucket_ids.transpose(1, 2, 0)
    vocab = lax.broadcasted_iota(jnp.int32, ids.shape, 0)
    turned = ((ids >> 9) ^ vocab) & 1
    away = ((ids >> 8) & 1) ^ core
    places = turned * (2 * HALF) + away * HALF + (ids >> 10) * 256 + (ids & 255)
    used = lax.broadcasted_iota(jnp.int32, ids.shape, 1) < bag_lengths.T[:, None, :]
    places = jnp.where(used, places, 4 * HALF)
    scores = pl.pallas_call(
        score_kernel,
        out_shape=jax.ShapeDtypeStruct((8, 256), F32),
        in_specs=[SMEM] + [VMEM] * 5,
        out_specs=VMEM,
        scratch_shapes=[pltpu.VMEM((4 * HALF + 8, 128), F32), pltpu.VMEM((12, 256, 128), F32)],
        compiler_params=PARAMS,
        name="score",
    )(places, own, other, weights, b_hidden[None, :], w_score[None, :])
    return (table_out.T, accum_out.T, scores[0])


def solution(mesh):
    shards = ("x", "z")
    every = ("y", "c", "x", "z")
    inner = Mesh(mesh.devices.reshape(8, 2, 4, 8), every)
    return jax.shard_map(
        per_device,
        mesh=inner,
        in_specs=(
            P(shards, None),
            P(shards, None),
            P(every, None),
            P(every),
            P(every),
            P(every, None, None),
            P(every, None),
            P(shards, None),
            P(),
            P(),
        ),
        out_specs=(P(shards, None), P(shards, None), P(every)),
        check_vma=False,
    )
```

```python
import jax
import jax.numpy as jnp
from jax import lax
from jax.experimental import pallas as pl
from jax.experimental.pallas import tpu as pltpu
from jax.sharding import Mesh
from jax.sharding import PartitionSpec as P

BF = jnp.bfloat16
F32 = jnp.float32
VMEM = pl.BlockSpec(memory_space=pltpu.VMEM)
HBM = pl.BlockSpec(memory_space=pltpu.HBM)
SMEM = pl.BlockSpec(memory_space=pltpu.SMEM)
HALF = 8192
PARAMS = pltpu.CompilerParams(vmem_limit_bytes=56 * 2**20)


def message_kernel(values_t, rows, counts, out):
    owners, slots = counts.shape[1], rows.shape[1]
    per_owner = slots // owners
    spread = (
        lax.broadcasted_iota(jnp.int32, (owners, slots), 0)
        == lax.broadcasted_iota(jnp.int32, (owners, slots), 1) // per_owner
    ).astype(BF)
    many = jnp.broadcast_to(counts[...].astype(F32), (8, owners)).astype(BF)
    live = jnp.dot(many, spread, preferred_element_type=F32)
    place = lax.broadcasted_iota(jnp.int32, (1, slots), 1) % per_owner
    target = jnp.where(place < live[:1].astype(jnp.int32), rows[...], -64)
    high = jnp.broadcast_to(target >> 5, (64, slots)).astype(F32)
    low = jnp.broadcast_to(target & 31, (64, slots)).astype(F32)
    first = lax.broadcasted_iota(jnp.int32, (64, slots), 0) == 0
    digits = jnp.where(first, high, low)
    out[...] = jnp.concatenate([values_t[...], digits], axis=0).T.astype(BF)


def update_kernel(core, message, table_t, accum_t, table_out, accum_out, block):
    rows = table_t.shape[1]
    total = jnp.zeros((128, rows), F32)
    step = 512
    for start in range(0, message.shape[0], step):
        part = message[start : start + step]
        target = (part[:, 64:65].astype(F32) * 32.0 + part[:, 65:66].astype(F32)).astype(jnp.int32)
        picks = (target == lax.broadcasted_iota(jnp.int32, (step, rows), 1)).astype(F32).astype(BF)
        total += lax.dot_general(part, picks, (((0,), (0,)), ((), ())), preferred_element_type=F32)
    grad = total[:64]
    accum_new = accum_t[...] + grad * grad
    table_new = table_t[...] - 0.5 * grad * lax.rsqrt(accum_new)
    accum_out[...] = accum_new
    table_out[...] = table_new
    stacked = jnp.concatenate([table_new[:, : rows // 2], table_new[:, rows // 2 :]], axis=0)
    mine = jnp.where(core[0] == 0, stacked[:, : rows // 4], stacked[:, rows // 4 :])
    serving = mine.T.astype(BF)
    for i in range(block.shape[0]):
        block[i] = serving


def score_kernel(ids_in, own, other, weights_in, bias, head, out, ids, rows, pooled, staged, weights, table_sems, id_sem, weight_sem):
    step = 2048
    id_copy = pltpu.make_async_copy(ids_in, ids, id_sem)
    id_copy.start()
    copies = []
    for k, half in enumerate((own, other)):
        for start in range(0, HALF, step):
            copies.append(
                pltpu.make_async_copy(
                    half.at[pl.ds(start, step)],
                    staged.at[pl.ds(k * HALF + start, step)],
                    table_sems.at[len(copies)],
                )
            )
            copies[-1].start()
    weight_copy = pltpu.make_async_copy(weights_in, weights, weight_sem)
    weight_copy.start()
    for i, copy in enumerate(copies):
        copy.wait()
        value = staged[i * step : (i + 1) * step].astype(F32)
        rows[i * step : (i + 1) * step] = value
        rows[2 * HALF + i * step : 2 * HALF + (i + 1) * step] = pltpu.roll(value, 64, 1)
    rows[4 * HALF : 4 * HALF + 8] = jnp.zeros((8, 128), F32)
    left = lax.broadcasted_iota(jnp.int32, (1, 128), 1) < 64
    pairs, requests, _ = pooled.shape
    id_copy.wait()

    def bag(vocab, r):
        at = 2 * vocab * requests + r
        return rows[pl.ds(ids[at], 1), :] + rows[pl.ds(ids[at + requests], 1), :]

    def look_up(r, carry):
        for j in range(pairs):
            pooled[j, pl.ds(r, 1), :] = jnp.where(left, bag(2 * j, r), bag(2 * j + 1, r))
        return carry

    lax.fori_loop(0, requests, look_up, 0, unroll=2)
    features = jnp.concatenate([pooled[j].astype(BF) for j in range(pairs)], axis=1)
    weight_copy.wait()
    unit = jnp.dot(features, weights[...], preferred_element_type=F32) + bias[...]
    hidden = (unit / (1.0 + jnp.exp(-unit))).astype(BF)
    heads = jnp.broadcast_to(head[...].astype(F32), (8, head.shape[1])).astype(BF)
    scores = lax.dot_general(heads, hidden, (((1,), (1,)), ((), ())), preferred_element_type=F32)
    out[...] = scores[0]


def per_device(
    table,
    accum,
    grad_values,
    grad_rows,
    grad_counts,
    bucket_ids,
    bag_lengths,
    w_hidden,
    b_hidden,
    w_score,
):
    core = lax.axis_index("c")
    weights = lax.all_gather(w_hidden, ("x", "z"), axis=0, tiled=True)
    message = pl.pallas_call(
        message_kernel,
        out_shape=jax.ShapeDtypeStruct((128, 128), BF),
        in_specs=[VMEM] * 3,
        out_specs=VMEM,
        name="message",
    )(grad_values.T, grad_rows[None, :], grad_counts[None, :])
    got = lax.all_to_all(message.reshape(32, 4, 128), ("x", "z"), 0, 0, tiled=True)
    slots = lax.all_gather(got, ("y", "c"), axis=0, tiled=True).reshape(2048, 128)
    table_out, accum_out, block = pl.pallas_call(
        update_kernel,
        out_shape=(
            jax.ShapeDtypeStruct((64, 1024), F32),
            jax.ShapeDtypeStruct((64, 1024), F32),
            jax.ShapeDtypeStruct((8, 256, 128), BF),
        ),
        in_specs=[SMEM] + [VMEM] * 3,
        out_specs=(VMEM,) * 3,
        compiler_params=PARAMS,
        name="update",
    )(core[None], slots, table.T, accum.T)
    column = lax.all_to_all(block, "z", 0, 0, tiled=True).reshape(1, 2048, 128)
    own = lax.all_to_all(jnp.broadcast_to(column, (4, 2048, 128)), "x", 0, 0, tiled=True).reshape(HALF, 128)
    other = lax.ppermute(own, "c", [(0, 1), (1, 0)])

    ids = bucket_ids.transpose(1, 2, 0)
    vocab = lax.broadcasted_iota(jnp.int32, ids.shape, 0)
    turned = ((ids >> 9) ^ vocab) & 1
    away = ((ids >> 8) & 1) ^ core
    places = turned * (2 * HALF) + away * HALF + (ids >> 10) * 256 + (ids & 255)
    used = lax.broadcasted_iota(jnp.int32, ids.shape, 1) < bag_lengths.T[:, None, :]
    places = jnp.where(used, places, 4 * HALF)
    scores = pl.pallas_call(
        score_kernel,
        out_shape=jax.ShapeDtypeStruct((256,), F32),
        in_specs=[HBM] * 4 + [VMEM] * 2,
        out_specs=VMEM,
        scratch_shapes=[
            pltpu.SMEM((12288,), jnp.int32),
            pltpu.VMEM((4 * HALF + 8, 128), F32),
            pltpu.VMEM((12, 256, 128), F32),
            pltpu.VMEM((2 * HALF, 128), BF),
            pltpu.VMEM((1536, 1024), BF),
            pltpu.SemaphoreType.DMA((8,)),
            pltpu.SemaphoreType.DMA,
            pltpu.SemaphoreType.DMA,
        ],
        compiler_params=PARAMS,
        name="score",
    )(places.reshape(-1), own, other, weights, b_hidden[None, :], w_score[None, :])
    return (table_out.T, accum_out.T, scores)


def solution(mesh):
    shards = ("x", "z")
    every = ("y", "c", "x", "z")
    inner = Mesh(mesh.devices.reshape(8, 2, 4, 8), every)
    return jax.shard_map(
        per_device,
        mesh=inner,
        in_specs=(
            P(shards, None),
            P(shards, None),
            P(every, None),
            P(every),
            P(every),
            P(every, None, None),
            P(every, None),
            P(shards, None),
            P(),
            P(),
        ),
        out_specs=(P(shards, None), P(shards, None), P(every)),
        check_vma=False,
    )
```

```python
import jax
import jax.numpy as jnp
from jax import lax
from jax.experimental import pallas as pl
from jax.experimental.pallas import tpu as pltpu
from jax.sharding import Mesh
from jax.sharding import PartitionSpec as P

BF = jnp.bfloat16
F32 = jnp.float32
VMEM = pl.BlockSpec(memory_space=pltpu.VMEM)
HBM = pl.BlockSpec(memory_space=pltpu.HBM)
ANY = pl.BlockSpec(memory_space=pl.ANY)
SMEM = pl.BlockSpec(memory_space=pltpu.SMEM)
HALF = 8192
SMALL = pltpu.CompilerParams(vmem_limit_bytes=36 * 2**20)
LARGE = pltpu.CompilerParams(vmem_limit_bytes=48 * 2**20)


def message_kernel(part, values_t, rows, counts, weights, out, quarters):
    owners, slots = counts.shape[1], rows.shape[1]
    per_owner = slots // owners
    spread = (
        lax.broadcasted_iota(jnp.int32, (owners, slots), 0)
        == lax.broadcasted_iota(jnp.int32, (owners, slots), 1) // per_owner
    ).astype(BF)
    many = jnp.broadcast_to(counts[...].astype(F32), (8, owners)).astype(BF)
    live = jnp.dot(many, spread, preferred_element_type=F32)
    place = lax.broadcasted_iota(jnp.int32, (1, slots), 1) % per_owner
    target = jnp.where(place < live[:1].astype(jnp.int32), rows[...], -64)
    high = jnp.broadcast_to(target >> 5, (64, slots)).astype(F32)
    low = jnp.broadcast_to(target & 31, (64, slots)).astype(F32)
    first = lax.broadcasted_iota(jnp.int32, (64, slots), 0) == 0
    digits = jnp.where(first, high, low)
    out[...] = jnp.concatenate([values_t[...], digits], axis=0).T.astype(BF)
    width = quarters.shape[2]
    mine = weights[:, pl.ds(pl.multiple_of(part[0] * width, width), width)]
    for i in range(quarters.shape[0]):
        quarters[i] = mine


def update_kernel(core, message, state, table_out, accum_out, block):
    rows = state.shape[1]
    total = jnp.zeros((128, rows), F32)
    step = 512
    for start in range(0, message.shape[0], step):
        part = message[start : start + step]
        target = (part[:, 64:65].astype(F32) * 32.0 + part[:, 65:66].astype(F32)).astype(jnp.int32)
        picks = (target == lax.broadcasted_iota(jnp.int32, (step, rows), 1)).astype(F32).astype(BF)
        total += lax.dot_general(part, picks, (((0,), (0,)), ((), ())), preferred_element_type=F32)
    grad = total[:64]
    accum_new = state[64:] + grad * grad
    table_new = state[:64] - 0.5 * grad * lax.rsqrt(accum_new)
    accum_out[...] = accum_new
    table_out[...] = table_new
    stacked = jnp.concatenate([table_new[:, : rows // 2], table_new[:, rows // 2 :]], axis=0)
    mine = jnp.where(core[0] == 0, stacked[:, : rows // 4], stacked[:, rows // 4 :])
    serving = mine.T.astype(BF)
    for i in range(block.shape[0]):
        block[i] = serving


def score_kernel(part, ids_in, own, other, weights_in, bias, head, out, rows, pooled, weights, weight_sems, id_sems, *ids):
    requests = pooled.shape[1]
    id_copies = [
        pltpu.make_async_copy(ids_in.at[pl.ds(i * requests, requests)], to, id_sems.at[i])
        for i, to in enumerate(ids)
    ]
    depth, width = weights.shape[0], weights.shape[1] // 4
    weight_copies = [
        pltpu.make_async_copy(
            weights_in.at[pl.ds(i * depth, depth)],
            weights.at[:, pl.ds(i * width, width)],
            weight_sems.at[i],
        )
        for i in range(4)
    ]
    for copy in id_copies + weight_copies:
        copy.start()
    step = 2048
    for half, at in ((own, 0), (other, HALF)):
        for start in range(0, HALF, step):
            value = half[start : start + step].astype(F32)
            rows[at + start : at + start + step] = value
            rows[2 * HALF + at + start : 2 * HALF + at + start + step] = pltpu.roll(value, 64, 1)
    rows[4 * HALF : 4 * HALF + 8] = jnp.zeros((8, 128), F32)
    left = lax.broadcasted_iota(jnp.int32, (1, 128), 1) < 64
    pairs = pooled.shape[0]
    for copy in id_copies:
        copy.wait()

    def bag(vocab, r):
        return rows[pl.ds(ids[2 * vocab][r], 1), :] + rows[pl.ds(ids[2 * vocab + 1][r], 1), :]

    def look_up(r, carry):
        for j in range(pairs):
            pooled[j, pl.ds(r, 1), :] = jnp.where(left, bag(2 * j, r), bag(2 * j + 1, r))
        return carry

    lax.fori_loop(0, requests, look_up, 0, unroll=4)
    features = jnp.concatenate([pooled[j].astype(BF) for j in range(pairs)], axis=1)
    columns = [pl.ds(pl.multiple_of((part[0] ^ i) * width, width), width) for i in range(4)]
    offset = jnp.concatenate([bias[:, at] for at in columns], axis=1)
    heads = jnp.concatenate([head[:, at].astype(F32) for at in columns], axis=1)
    heads = jnp.broadcast_to(heads, (8, heads.shape[1])).astype(BF)
    for copy in weight_copies:
        copy.wait()
    unit = jnp.dot(features, weights[...], preferred_element_type=F32) + offset
    hidden = (unit / (1.0 + jnp.exp(-unit))).astype(BF)
    scores = lax.dot_general(heads, hidden, (((1,), (1,)), ((), ())), preferred_element_type=F32)
    out[...] = scores[0]


def shift(value, axis, by):
    size = lax.axis_size(axis)
    return lax.ppermute(value, axis, [(i, (i + by) % size) for i in range(size)])


def per_device(
    table,
    accum,
    grad_values,
    grad_rows,
    grad_counts,
    bucket_ids,
    bag_lengths,
    w_hidden,
    b_hidden,
    w_score,
):
    core = lax.axis_index("c")
    part = core * 2 + lax.axis_index("y") % 2
    state = jnp.concatenate([table.T, accum.T], axis=0)
    message, quarters = pl.pallas_call(
        message_kernel,
        out_shape=(jax.ShapeDtypeStruct((128, 128), BF), jax.ShapeDtypeStruct((32, 48, 256), BF)),
        in_specs=[SMEM] + [VMEM] * 4,
        out_specs=(VMEM,) * 2,
        name="message",
    )(part[None], grad_values.T, grad_rows[None, :], grad_counts[None, :], w_hidden)
    got = lax.all_to_all(message.reshape(32, 4, 128), ("x", "z"), 0, 0, tiled=True)
    got, quarters, state = lax.optimization_barrier((got, quarters, state))
    first = lax.all_to_all(quarters, ("x", "z"), 0, 0, tiled=True).reshape(1536, 256)
    slots = lax.all_gather(got, ("y", "c"), axis=0, tiled=True).reshape(2048, 128)
    table_out, accum_out, block = pl.pallas_call(
        update_kernel,
        out_shape=(
            jax.ShapeDtypeStruct((64, 1024), F32),
            jax.ShapeDtypeStruct((64, 1024), F32),
            jax.ShapeDtypeStruct((8, 256, 128), BF),
        ),
        in_specs=[SMEM, VMEM, VMEM],
        out_specs=(VMEM,) * 3,
        compiler_params=SMALL,
        name="update",
    )(core[None], slots, state)
    block, first = lax.optimization_barrier((block, first))
    column = lax.all_to_all(block, "z", 0, 0, tiled=True).reshape(2048, 128)
    upper, lower = shift(first[:768], "y", 1), shift(first[768:], "y", 7)
    column, first, upper, lower = lax.optimization_barrier((column, first, upper, lower))
    swapped = [shift(piece, "c", 1) for piece in (first, upper, lower)]
    columns = jnp.broadcast_to(column[None], (4, 2048, 128))
    own = lax.all_to_all(columns, "x", 0, 0, tiled=True).reshape(HALF, 128)
    weights = jnp.concatenate([first, upper, lower, *swapped], axis=0)
    own, weights = lax.optimization_barrier((own, weights))
    other = shift(own, "c", 1)

    ids = bucket_ids.transpose(1, 2, 0)
    vocab = lax.broadcasted_iota(jnp.int32, ids.shape, 0)
    turned = ((ids >> 9) ^ vocab) & 1
    away = ((ids >> 8) & 1) ^ core
    places = turned * (2 * HALF) + away * HALF + (ids >> 10) * 256 + (ids & 255)
    used = lax.broadcasted_iota(jnp.int32, ids.shape, 1) < bag_lengths.T[:, None, :]
    places = jnp.where(used, places, 4 * HALF)
    scores = pl.pallas_call(
        score_kernel,
        out_shape=jax.ShapeDtypeStruct((256,), F32),
        in_specs=[SMEM] + [HBM] + [VMEM] * 2 + [ANY] + [VMEM] * 2,
        out_specs=VMEM,
        scratch_shapes=[
            pltpu.VMEM((4 * HALF + 8, 128), F32),
            pltpu.VMEM((12, 256, 128), F32),
            pltpu.VMEM((1536, 1024), BF),
            pltpu.SemaphoreType.DMA((4,)),
            pltpu.SemaphoreType.DMA((48,)),
        ]
        + [pltpu.SMEM((256,), jnp.int32)] * 48,
        compiler_params=LARGE,
        name="score",
    )(
        part[None],
        places.reshape(-1),
        own,
        other,
        weights,
        b_hidden[None, :],
        w_score[None, :],
    )
    return (table_out.T, accum_out.T, scores)


def solution(mesh):
    shards = ("x", "z")
    every = ("y", "c", "x", "z")
    inner = Mesh(mesh.devices.reshape(8, 2, 4, 8), every)
    return jax.shard_map(
        per_device,
        mesh=inner,
        in_specs=(
            P(shards, None),
            P(shards, None),
            P(every, None),
            P(every),
            P(every),
            P(every, None, None),
            P(every, None),
            P(shards, None),
            P(),
            P(),
        ),
        out_specs=(P(shards, None), P(shards, None), P(every)),
        check_vma=False,
    )
```

```python
import jax
import jax.numpy as jnp
from jax import lax
from jax.experimental import pallas as pl
from jax.experimental.pallas import tpu as pltpu
from jax.sharding import Mesh
from jax.sharding import PartitionSpec as P

BF = jnp.bfloat16
F32 = jnp.float32
VMEM = pl.BlockSpec(memory_space=pltpu.VMEM)
HBM = pl.BlockSpec(memory_space=pltpu.HBM)
ANY = pl.BlockSpec(memory_space=pl.ANY)
SMEM = pl.BlockSpec(memory_space=pltpu.SMEM)
HALF = 8192
SMALL = pltpu.CompilerParams(vmem_limit_bytes=36 * 2**20)
LARGE = pltpu.CompilerParams(vmem_limit_bytes=48 * 2**20)


def message_kernel(part, values_t, rows, counts, weights, out, quarters):
    owners, slots = counts.shape[1], rows.shape[1]
    per_owner = slots // owners
    spread = (
        lax.broadcasted_iota(jnp.int32, (owners, slots), 0)
        == lax.broadcasted_iota(jnp.int32, (owners, slots), 1) // per_owner
    ).astype(BF)
    many = jnp.broadcast_to(counts[...].astype(F32), (8, owners)).astype(BF)
    live = jnp.dot(many, spread, preferred_element_type=F32)
    place = lax.broadcasted_iota(jnp.int32, (1, slots), 1) % per_owner
    target = jnp.where(place < live[:1].astype(jnp.int32), rows[...], -64)
    high = jnp.broadcast_to(target >> 5, (64, slots)).astype(F32)
    low = jnp.broadcast_to(target & 31, (64, slots)).astype(F32)
    first = lax.broadcasted_iota(jnp.int32, (64, slots), 0) == 0
    digits = jnp.where(first, high, low)
    out[...] = jnp.concatenate([values_t[...], digits], axis=0).T.astype(BF)
    width = quarters.shape[2]
    mine = weights[:, pl.ds(pl.multiple_of(part[0] * width, width), width)]
    for i in range(quarters.shape[0]):
        quarters[i] = mine


def update_kernel(core, message, state, table_out, accum_out, block):
    rows = state.shape[1]
    total = jnp.zeros((128, rows), F32)
    step = 512
    for start in range(0, message.shape[0], step):
        part = message[start : start + step]
        target = (part[:, 64:65].astype(F32) * 32.0 + part[:, 65:66].astype(F32)).astype(jnp.int32)
        picks = (target == lax.broadcasted_iota(jnp.int32, (step, rows), 1)).astype(F32).astype(BF)
        total += lax.dot_general(part, picks, (((0,), (0,)), ((), ())), preferred_element_type=F32)
    grad = total[:64]
    accum_new = state[64:] + grad * grad
    table_new = state[:64] - 0.5 * grad * lax.rsqrt(accum_new)
    accum_out[...] = accum_new
    table_out[...] = table_new
    stacked = jnp.concatenate([table_new[:, : rows // 2], table_new[:, rows // 2 :]], axis=0)
    mine = jnp.where(core[0] == 0, stacked[:, : rows // 4], stacked[:, rows // 4 :])
    serving = mine.T.astype(BF)
    for i in range(block.shape[0]):
        block[i] = serving


def score_kernel(part, ids_in, own, other, weights_in, bias, head, out, rows, pooled, weights, weight_sems, id_sems, *ids):
    requests = pooled.shape[1]
    id_copies = [
        pltpu.make_async_copy(ids_in.at[pl.ds(i * requests, requests)], to, id_sems.at[i])
        for i, to in enumerate(ids)
    ]
    depth, width = weights.shape[0], weights.shape[1] // 4
    weight_copies = [
        pltpu.make_async_copy(
            weights_in.at[pl.ds(i * depth, depth)],
            weights.at[:, pl.ds(i * width, width)],
            weight_sems.at[i],
        )
        for i in range(4)
    ]
    for copy in id_copies + weight_copies:
        copy.start()
    step = 2048
    for half, at in ((own, 0), (other, HALF)):
        for start in range(0, HALF, step):
            value = half[start : start + step].astype(F32)
            rows[at + start : at + start + step] = value
            rows[2 * HALF + at + start : 2 * HALF + at + start + step] = pltpu.roll(value, 64, 1)
    rows[4 * HALF : 4 * HALF + 8] = jnp.zeros((8, 128), F32)
    left = lax.broadcasted_iota(jnp.int32, (1, 128), 1) < 64
    pairs = pooled.shape[0]
    for copy in id_copies:
        copy.wait()

    def bag(vocab, r):
        return rows[pl.ds(ids[2 * vocab][r], 1), :] + rows[pl.ds(ids[2 * vocab + 1][r], 1), :]

    def look_up(r, carry):
        for j in range(pairs):
            pooled[j, pl.ds(r, 1), :] = jnp.where(left, bag(2 * j, r), bag(2 * j + 1, r))
        return carry

    lax.fori_loop(0, requests, look_up, 0, unroll=4)
    features = jnp.concatenate([pooled[j].astype(BF) for j in range(pairs)], axis=1)
    columns = [pl.ds(pl.multiple_of((part[0] ^ i) * width, width), width) for i in range(4)]
    offset = jnp.concatenate([bias[:, at] for at in columns], axis=1)
    heads = jnp.concatenate([head[:, at].astype(F32) for at in columns], axis=1)
    heads = jnp.broadcast_to(heads, (8, heads.shape[1])).astype(BF)
    for copy in weight_copies:
        copy.wait()
    unit = jnp.dot(features, weights[...], preferred_element_type=F32) + offset
    hidden = (unit / (1.0 + jnp.exp(-unit))).astype(BF)
    scores = lax.dot_general(heads, hidden, (((1,), (1,)), ((), ())), preferred_element_type=F32)
    out[...] = scores[0]


def shift(value, axis, by):
    size = lax.axis_size(axis)
    return lax.ppermute(value, axis, [(i, (i + by) % size) for i in range(size)])


def per_device(
    table,
    accum,
    grad_values,
    grad_rows,
    grad_counts,
    bucket_ids,
    bag_lengths,
    w_hidden,
    b_hidden,
    w_score,
):
    core = lax.axis_index("c")
    part = core * 2 + lax.axis_index("y") % 2
    state = jnp.concatenate([table.T, accum.T], axis=0)
    message, quarters = pl.pallas_call(
        message_kernel,
        out_shape=(jax.ShapeDtypeStruct((128, 128), BF), jax.ShapeDtypeStruct((32, 48, 256), BF)),
        in_specs=[SMEM] + [VMEM] * 4,
        out_specs=(VMEM,) * 2,
        name="message",
    )(part[None], grad_values.T, grad_rows[None, :], grad_counts[None, :], w_hidden)
    got = lax.all_to_all(message.reshape(32, 4, 128), ("x", "z"), 0, 0, tiled=True)
    got, quarters, state = lax.optimization_barrier((got, quarters, state))
    first = lax.all_to_all(quarters, ("x", "z"), 0, 0, tiled=True).reshape(1536, 256)
    slots = lax.all_gather(got, ("y", "c"), axis=0, tiled=True).reshape(2048, 128)
    table_out, accum_out, block = pl.pallas_call(
        update_kernel,
        out_shape=(
            jax.ShapeDtypeStruct((64, 1024), F32),
            jax.ShapeDtypeStruct((64, 1024), F32),
            jax.ShapeDtypeStruct((8, 256, 128), BF),
        ),
        in_specs=[SMEM, VMEM, VMEM],
        out_specs=(VMEM,) * 3,
        compiler_params=SMALL,
        name="update",
    )(core[None], slots, state)
    block, first = lax.optimization_barrier((block, first))
    column = lax.all_to_all(block, "z", 0, 0, tiled=True).reshape(2048, 128)
    column, first = lax.optimization_barrier((column, first))
    upper, lower = shift(first[:768], "y", 1), shift(first[768:], "y", 7)
    swapped = [shift(piece, "c", 1) for piece in (first, upper, lower)]
    columns = jnp.broadcast_to(column[None], (4, 2048, 128))
    own = lax.all_to_all(columns, "x", 0, 0, tiled=True).reshape(HALF, 128)
    weights = jnp.concatenate([first, upper, lower, *swapped], axis=0)
    own, weights = lax.optimization_barrier((own, weights))
    other = shift(own, "c", 1)

    ids = bucket_ids.transpose(1, 2, 0)
    vocab = lax.broadcasted_iota(jnp.int32, ids.shape, 0)
    turned = ((ids >> 9) ^ vocab) & 1
    away = ((ids >> 8) & 1) ^ core
    places = turned * (2 * HALF) + away * HALF + (ids >> 10) * 256 + (ids & 255)
    used = lax.broadcasted_iota(jnp.int32, ids.shape, 1) < bag_lengths.T[:, None, :]
    places = jnp.where(used, places, 4 * HALF)
    scores = pl.pallas_call(
        score_kernel,
        out_shape=jax.ShapeDtypeStruct((256,), F32),
        in_specs=[SMEM] + [HBM] + [VMEM] * 2 + [ANY] + [VMEM] * 2,
        out_specs=VMEM,
        scratch_shapes=[
            pltpu.VMEM((4 * HALF + 8, 128), F32),
            pltpu.VMEM((12, 256, 128), F32),
            pltpu.VMEM((1536, 1024), BF),
            pltpu.SemaphoreType.DMA((4,)),
            pltpu.SemaphoreType.DMA((48,)),
        ]
        + [pltpu.SMEM((256,), jnp.int32)] * 48,
        compiler_params=LARGE,
        name="score",
    )(
        part[None],
        places.reshape(-1),
        own,
        other,
        weights,
        b_hidden[None, :],
        w_score[None, :],
    )
    return (table_out.T, accum_out.T, scores)


def solution(mesh):
    shards = ("x", "z")
    every = ("y", "c", "x", "z")
    inner = Mesh(mesh.devices.reshape(8, 2, 4, 8), every)
    return jax.shard_map(
        per_device,
        mesh=inner,
        in_specs=(
            P(shards, None),
            P(shards, None),
            P(every, None),
            P(every),
            P(every),
            P(every, None, None),
            P(every, None),
            P(shards, None),
            P(),
            P(),
        ),
        out_specs=(P(shards, None), P(shards, None), P(every)),
        check_vma=False,
    )
```

```python
import jax
import jax.numpy as jnp
from jax import lax
from jax.experimental import pallas as pl
from jax.experimental.pallas import tpu as pltpu
from jax.sharding import Mesh
from jax.sharding import PartitionSpec as P

BF = jnp.bfloat16
F32 = jnp.float32
VMEM = pl.BlockSpec(memory_space=pltpu.VMEM)
HBM = pl.BlockSpec(memory_space=pltpu.HBM)
ANY = pl.BlockSpec(memory_space=pl.ANY)
SMEM = pl.BlockSpec(memory_space=pltpu.SMEM)
HALF = 8192
SMALL = pltpu.CompilerParams(vmem_limit_bytes=36 * 2**20)
LARGE = pltpu.CompilerParams(vmem_limit_bytes=48 * 2**20)


def message_kernel(part, values_t, rows, counts, weights, out, quarters):
    owners, slots = counts.shape[1], rows.shape[1]
    per_owner = slots // owners
    spread = (
        lax.broadcasted_iota(jnp.int32, (owners, slots), 0)
        == lax.broadcasted_iota(jnp.int32, (owners, slots), 1) // per_owner
    ).astype(BF)
    many = jnp.broadcast_to(counts[...].astype(F32), (8, owners)).astype(BF)
    live = jnp.dot(many, spread, preferred_element_type=F32)
    place = lax.broadcasted_iota(jnp.int32, (1, slots), 1) % per_owner
    target = jnp.where(place < live[:1].astype(jnp.int32), rows[...], -64)
    high = jnp.broadcast_to(target >> 5, (64, slots)).astype(F32)
    low = jnp.broadcast_to(target & 31, (64, slots)).astype(F32)
    first = lax.broadcasted_iota(jnp.int32, (64, slots), 0) == 0
    digits = jnp.where(first, high, low)
    out[...] = jnp.concatenate([values_t[...], digits], axis=0).T.astype(BF)
    width = quarters.shape[2]
    mine = weights[:, pl.ds(pl.multiple_of(part[0] * width, width), width)]
    for i in range(quarters.shape[0]):
        quarters[i] = mine


def pack_kernel(slots, out):
    value = slots[...].astype(F32)
    left = lax.broadcasted_iota(jnp.int32, (64, 128), 1) < 64
    out[:64] = jnp.where(left, value[:64], pltpu.roll(value[64:], 64, 1)).astype(BF)
    out[64:] = value.T[64:80].astype(BF)


def update_kernel(core, message, state, table_out, accum_out, block):
    rows = state.shape[1]
    total = jnp.zeros((128, rows), F32)
    left = lax.broadcasted_iota(jnp.int32, (1, 128), 1) < 64
    row = lax.broadcasted_iota(jnp.int32, (rows, 128), 0).astype(F32)
    for start in range(0, message.shape[0], 160):
        values = [message[at : at + 64].astype(F32) for at in (start, start + 80)]
        digits = [message[at : at + 16].astype(F32) for at in (start + 64, start + 144)]
        one, two = (part[0:1] * 32.0 + part[1:2] for part in digits)
        values = jnp.concatenate(values, axis=0)
        values = jnp.concatenate([values, pltpu.roll(values, 64, 1)], axis=0).astype(BF)
        first = jnp.where(left, one, pltpu.roll(two, 64, 1))
        second = jnp.where(left, pltpu.roll(one, 64, 1), two)
        picks = jnp.concatenate([(row == target).astype(F32).astype(BF) for target in (first, second)], axis=1)
        total += lax.dot_general(values, picks, (((0,), (1,)), ((), ())), preferred_element_type=F32)
    grad = total[:64]
    accum_new = state[64:] + grad * grad
    table_new = state[:64] - 0.5 * grad * lax.rsqrt(accum_new)
    accum_out[...] = accum_new
    table_out[...] = table_new
    stacked = jnp.concatenate([table_new[:, : rows // 2], table_new[:, rows // 2 :]], axis=0)
    mine = jnp.where(core[0] == 0, stacked[:, : rows // 4], stacked[:, rows // 4 :])
    serving = mine.T.astype(BF)
    for i in range(block.shape[0]):
        block[i] = serving


def score_kernel(part, ids_in, own, other, weights_in, bias, head, out, rows, pooled, weights, weight_sems, id_sems, *ids):
    requests = pooled.shape[1]
    id_copies = [
        pltpu.make_async_copy(ids_in.at[pl.ds(i * requests, requests)], to, id_sems.at[i])
        for i, to in enumerate(ids)
    ]
    depth, width = weights.shape[0], weights.shape[1] // 4
    weight_copies = [
        pltpu.make_async_copy(
            weights_in.at[pl.ds(i * depth, depth)],
            weights.at[:, pl.ds(i * width, width)],
            weight_sems.at[i],
        )
        for i in range(4)
    ]
    for copy in id_copies + weight_copies:
        copy.start()
    step = 2048
    for half, at in ((own, 0), (other, HALF)):
        for start in range(0, HALF, step):
            value = half[start : start + step].astype(F32)
            rows[at + start : at + start + step] = value
            rows[2 * HALF + at + start : 2 * HALF + at + start + step] = pltpu.roll(value, 64, 1)
    rows[4 * HALF : 4 * HALF + 8] = jnp.zeros((8, 128), F32)
    left = lax.broadcasted_iota(jnp.int32, (1, 128), 1) < 64
    pairs = pooled.shape[0]
    for copy in id_copies:
        copy.wait()

    def bag(vocab, r):
        return rows[pl.ds(ids[2 * vocab][r], 1), :] + rows[pl.ds(ids[2 * vocab + 1][r], 1), :]

    def look_up(r, carry):
        for j in range(pairs):
            pooled[j, pl.ds(r, 1), :] = jnp.where(left, bag(2 * j, r), bag(2 * j + 1, r))
        return carry

    lax.fori_loop(0, requests, look_up, 0, unroll=8)
    features = jnp.concatenate([pooled[j].astype(BF) for j in range(pairs)], axis=1)
    columns = [pl.ds(pl.multiple_of((part[0] ^ i) * width, width), width) for i in range(4)]
    offset = jnp.concatenate([bias[:, at] for at in columns], axis=1)
    heads = jnp.concatenate([head[:, at].astype(F32) for at in columns], axis=1)
    heads = jnp.broadcast_to(heads, (8, heads.shape[1])).astype(BF)
    for copy in weight_copies:
        copy.wait()
    unit = jnp.dot(features, weights[...], preferred_element_type=F32) + offset
    hidden = (unit / (1.0 + jnp.exp(-unit))).astype(BF)
    scores = lax.dot_general(heads, hidden, (((1,), (1,)), ((), ())), preferred_element_type=F32)
    out[...] = scores[0]


def shift(value, axis, by):
    size = lax.axis_size(axis)
    return lax.ppermute(value, axis, [(i, (i + by) % size) for i in range(size)])


def per_device(
    table,
    accum,
    grad_values,
    grad_rows,
    grad_counts,
    bucket_ids,
    bag_lengths,
    w_hidden,
    b_hidden,
    w_score,
):
    core = lax.axis_index("c")
    part = core * 2 + lax.axis_index("y") % 2
    state = jnp.concatenate([table.T, accum.T], axis=0)
    message, quarters = pl.pallas_call(
        message_kernel,
        out_shape=(jax.ShapeDtypeStruct((128, 128), BF), jax.ShapeDtypeStruct((32, 48, 256), BF)),
        in_specs=[SMEM] + [VMEM] * 4,
        out_specs=(VMEM,) * 2,
        name="message",
    )(part[None], grad_values.T, grad_rows[None, :], grad_counts[None, :], w_hidden)
    got = lax.all_to_all(message.reshape(32, 4, 128), ("x", "z"), 0, 0, tiled=True)
    got, quarters, state = lax.optimization_barrier((got, quarters, state))
    first = lax.all_to_all(quarters, ("x", "z"), 0, 0, tiled=True).reshape(1536, 256)
    packed = pl.pallas_call(
        pack_kernel,
        out_shape=jax.ShapeDtypeStruct((80, 128), BF),
        in_specs=[VMEM],
        out_specs=VMEM,
        compiler_params=SMALL,
        name="pack",
    )(got.reshape(128, 128))
    slots = lax.all_gather(packed, ("y", "c"), axis=0, tiled=True)
    table_out, accum_out, block = pl.pallas_call(
        update_kernel,
        out_shape=(
            jax.ShapeDtypeStruct((64, 1024), F32),
            jax.ShapeDtypeStruct((64, 1024), F32),
            jax.ShapeDtypeStruct((8, 256, 128), BF),
        ),
        in_specs=[SMEM, VMEM, VMEM],
        out_specs=(VMEM,) * 3,
        compiler_params=SMALL,
        name="update",
    )(core[None], slots, state)
    block, first = lax.optimization_barrier((block, first))
    column = lax.all_to_all(block, "z", 0, 0, tiled=True).reshape(2048, 128)
    column, first = lax.optimization_barrier((column, first))
    upper, lower = shift(first[:768], "y", 1), shift(first[768:], "y", 7)
    swapped = [shift(piece, "c", 1) for piece in (first, upper, lower)]
    columns = jnp.broadcast_to(column[None], (4, 2048, 128))
    own = lax.all_to_all(columns, "x", 0, 0, tiled=True).reshape(HALF, 128)
    weights = jnp.concatenate([first, upper, lower, *swapped], axis=0)
    own, weights = lax.optimization_barrier((own, weights))
    other = shift(own, "c", 1)

    ids = bucket_ids.transpose(1, 2, 0)
    vocab = lax.broadcasted_iota(jnp.int32, ids.shape, 0)
    turned = ((ids >> 9) ^ vocab) & 1
    away = ((ids >> 8) & 1) ^ core
    places = turned * (2 * HALF) + away * HALF + (ids >> 10) * 256 + (ids & 255)
    used = lax.broadcasted_iota(jnp.int32, ids.shape, 1) < bag_lengths.T[:, None, :]
    places = jnp.where(used, places, 4 * HALF)
    scores = pl.pallas_call(
        score_kernel,
        out_shape=jax.ShapeDtypeStruct((256,), F32),
        in_specs=[SMEM] + [HBM] + [VMEM] * 2 + [ANY] + [VMEM] * 2,
        out_specs=VMEM,
        scratch_shapes=[
            pltpu.VMEM((4 * HALF + 8, 128), F32),
            pltpu.VMEM((12, 256, 128), F32),
            pltpu.VMEM((1536, 1024), BF),
            pltpu.SemaphoreType.DMA((4,)),
            pltpu.SemaphoreType.DMA((48,)),
        ]
        + [pltpu.SMEM((256,), jnp.int32)] * 48,
        compiler_params=LARGE,
        name="score",
    )(
        part[None],
        places.reshape(-1),
        own,
        other,
        weights,
        b_hidden[None, :],
        w_score[None, :],
    )
    return (table_out.T, accum_out.T, scores)


def solution(mesh):
    shards = ("x", "z")
    every = ("y", "c", "x", "z")
    inner = Mesh(mesh.devices.reshape(8, 2, 4, 8), every)
    return jax.shard_map(
        per_device,
        mesh=inner,
        in_specs=(
            P(shards, None),
            P(shards, None),
            P(every, None),
            P(every),
            P(every),
            P(every, None, None),
            P(every, None),
            P(shards, None),
            P(),
            P(),
        ),
        out_specs=(P(shards, None), P(shards, None), P(every)),
        check_vma=False,
    )
```

```python
import jax
import jax.numpy as jnp
from jax import lax
from jax.experimental import pallas as pl
from jax.experimental.pallas import tpu as pltpu
from jax.sharding import Mesh
from jax.sharding import PartitionSpec as P

BF = jnp.bfloat16
F32 = jnp.float32
VMEM = pl.BlockSpec(memory_space=pltpu.VMEM)
HBM = pl.BlockSpec(memory_space=pltpu.HBM)
ANY = pl.BlockSpec(memory_space=pl.ANY)
SMEM = pl.BlockSpec(memory_space=pltpu.SMEM)
HALF = 8192
SMALL = pltpu.CompilerParams(vmem_limit_bytes=36 * 2**20)
LARGE = pltpu.CompilerParams(vmem_limit_bytes=48 * 2**20)


def message_kernel(part, values_t, rows, counts, weights, out, quarters):
    owners, slots = counts.shape[1], rows.shape[1]
    per_owner = slots // owners
    spread = (
        lax.broadcasted_iota(jnp.int32, (owners, slots), 0)
        == lax.broadcasted_iota(jnp.int32, (owners, slots), 1) // per_owner
    ).astype(BF)
    many = jnp.broadcast_to(counts[...].astype(F32), (8, owners)).astype(BF)
    live = jnp.dot(many, spread, preferred_element_type=F32)
    place = lax.broadcasted_iota(jnp.int32, (1, slots), 1) % per_owner
    target = jnp.where(place < live[:1].astype(jnp.int32), rows[...], -64)
    high = jnp.broadcast_to(target >> 5, (64, slots)).astype(F32)
    low = jnp.broadcast_to(target & 31, (64, slots)).astype(F32)
    first = lax.broadcasted_iota(jnp.int32, (64, slots), 0) == 0
    digits = jnp.where(first, high, low)
    out[...] = jnp.concatenate([values_t[...], digits], axis=0).T.astype(BF)
    width = quarters.shape[2]
    mine = weights[:, pl.ds(pl.multiple_of(part[0] * width, width), width)]
    for i in range(quarters.shape[0]):
        quarters[i] = mine


def pack_kernel(slots, out):
    value = slots[...].astype(F32)
    left = lax.broadcasted_iota(jnp.int32, (64, 128), 1) < 64
    out[:64] = jnp.where(left, value[:64], pltpu.roll(value[64:], 64, 1)).astype(BF)
    out[64:] = value.T[64:80].astype(BF)


def update_kernel(core, message, state, table_out, accum_out, block):
    rows = state.shape[1]
    total = jnp.zeros((128, rows), F32)
    left = lax.broadcasted_iota(jnp.int32, (1, 128), 1) < 64
    row = lax.broadcasted_iota(jnp.int32, (rows, 128), 0).astype(F32)
    for start in range(0, message.shape[0], 160):
        values = [message[at : at + 64].astype(F32) for at in (start, start + 80)]
        digits = [message[at : at + 16].astype(F32) for at in (start + 64, start + 144)]
        one, two = (part[0:1] * 32.0 + part[1:2] for part in digits)
        values = jnp.concatenate(values, axis=0)
        values = jnp.concatenate([values, pltpu.roll(values, 64, 1)], axis=0).astype(BF)
        first = jnp.where(left, one, pltpu.roll(two, 64, 1))
        second = jnp.where(left, pltpu.roll(one, 64, 1), two)
        picks = jnp.concatenate([(row == target).astype(F32).astype(BF) for target in (first, second)], axis=1)
        total += lax.dot_general(values, picks, (((0,), (1,)), ((), ())), preferred_element_type=F32)
    grad = total[:64]
    accum_new = state[64:] + grad * grad
    table_new = state[:64] - 0.5 * grad * lax.rsqrt(accum_new)
    accum_out[...] = accum_new
    table_out[...] = table_new
    stacked = jnp.concatenate([table_new[:, : rows // 2], table_new[:, rows // 2 :]], axis=0)
    mine = jnp.where(core[0] == 0, stacked[:, : rows // 4], stacked[:, rows // 4 :])
    serving = mine.T.astype(BF)
    for i in range(block.shape[0]):
        block[i] = serving


def score_kernel(part, ids_in, own, other, weights_in, bias, head, out, rows, pooled, weights, weight_sems, id_sems, *ids):
    requests = pooled.shape[1]
    id_copies = [
        pltpu.make_async_copy(ids_in.at[pl.ds(i * requests, requests)], to, id_sems.at[i])
        for i, to in enumerate(ids)
    ]
    depth, width = weights.shape[0], weights.shape[1] // 4
    weight_copies = [
        pltpu.make_async_copy(
            weights_in.at[pl.ds(i * depth, depth)],
            weights.at[:, pl.ds(i * width, width)],
            weight_sems.at[i],
        )
        for i in range(4)
    ]
    for copy in id_copies + weight_copies:
        copy.start()
    step = 2048
    for half, at in ((own, 0), (other, HALF)):
        for start in range(0, HALF, step):
            value = half[start : start + step].astype(F32)
            rows[at + start : at + start + step] = value
            rows[2 * HALF + at + start : 2 * HALF + at + start + step] = pltpu.roll(value, 64, 1)
    rows[4 * HALF : 4 * HALF + 8] = jnp.zeros((8, 128), F32)
    left = lax.broadcasted_iota(jnp.int32, (1, 128), 1) < 64
    pairs = pooled.shape[0]
    for copy in id_copies:
        copy.wait()

    def bag(vocab, r):
        return rows[pl.ds(ids[2 * vocab][r], 1), :] + rows[pl.ds(ids[2 * vocab + 1][r], 1), :]

    def look_up(r, carry):
        for j in range(pairs):
            pooled[j, pl.ds(r, 1), :] = jnp.where(left, bag(2 * j, r), bag(2 * j + 1, r))
        return carry

    lax.fori_loop(0, requests, look_up, 0, unroll=16)
    features = jnp.concatenate([pooled[j].astype(BF) for j in range(pairs)], axis=1)
    columns = [pl.ds(pl.multiple_of((part[0] ^ i) * width, width), width) for i in range(4)]
    offset = jnp.concatenate([bias[:, at] for at in columns], axis=1)
    heads = jnp.concatenate([head[:, at].astype(F32) for at in columns], axis=1)
    heads = jnp.broadcast_to(heads, (8, heads.shape[1])).astype(BF)
    for copy in weight_copies:
        copy.wait()
    unit = jnp.dot(features, weights[...], preferred_element_type=F32) + offset
    hidden = (unit / (1.0 + jnp.exp(-unit))).astype(BF)
    scores = lax.dot_general(heads, hidden, (((1,), (1,)), ((), ())), preferred_element_type=F32)
    out[...] = scores[0]


def shift(value, axis, by):
    size = lax.axis_size(axis)
    return lax.ppermute(value, axis, [(i, (i + by) % size) for i in range(size)])


def per_device(
    table,
    accum,
    grad_values,
    grad_rows,
    grad_counts,
    bucket_ids,
    bag_lengths,
    w_hidden,
    b_hidden,
    w_score,
):
    core = lax.axis_index("c")
    part = core * 2 + lax.axis_index("y") % 2
    state = jnp.concatenate([table.T, accum.T], axis=0)
    message, quarters = pl.pallas_call(
        message_kernel,
        out_shape=(jax.ShapeDtypeStruct((128, 128), BF), jax.ShapeDtypeStruct((32, 48, 256), BF)),
        in_specs=[SMEM] + [VMEM] * 4,
        out_specs=(VMEM,) * 2,
        name="message",
    )(part[None], grad_values.T, grad_rows[None, :], grad_counts[None, :], w_hidden)
    got = lax.all_to_all(message.reshape(32, 4, 128), ("x", "z"), 0, 0, tiled=True)
    got, quarters, state = lax.optimization_barrier((got, quarters, state))
    first = lax.all_to_all(quarters, ("x", "z"), 0, 0, tiled=True).reshape(1536, 256)
    packed = pl.pallas_call(
        pack_kernel,
        out_shape=jax.ShapeDtypeStruct((80, 128), BF),
        in_specs=[VMEM],
        out_specs=VMEM,
        compiler_params=SMALL,
        name="pack",
    )(got.reshape(128, 128))
    slots = lax.all_gather(packed, ("y", "c"), axis=0, tiled=True)
    table_out, accum_out, block = pl.pallas_call(
        update_kernel,
        out_shape=(
            jax.ShapeDtypeStruct((64, 1024), F32),
            jax.ShapeDtypeStruct((64, 1024), F32),
            jax.ShapeDtypeStruct((8, 256, 128), BF),
        ),
        in_specs=[SMEM, VMEM, VMEM],
        out_specs=(VMEM,) * 3,
        compiler_params=SMALL,
        name="update",
    )(core[None], slots, state)
    block, first = lax.optimization_barrier((block, first))
    column = lax.all_to_all(block, "z", 0, 0, tiled=True).reshape(2048, 128)
    column, first = lax.optimization_barrier((column, first))
    upper, lower = shift(first[:768], "y", 1), shift(first[768:], "y", 7)
    swapped = [shift(piece, "c", 1) for piece in (first, upper, lower)]
    columns = jnp.broadcast_to(column[None], (4, 2048, 128))
    own = lax.all_to_all(columns, "x", 0, 0, tiled=True).reshape(HALF, 128)
    weights = jnp.concatenate([first, upper, lower, *swapped], axis=0)
    own, weights = lax.optimization_barrier((own, weights))
    other = shift(own, "c", 1)

    ids = bucket_ids.transpose(1, 2, 0)
    vocab = lax.broadcasted_iota(jnp.int32, ids.shape, 0)
    turned = ((ids >> 9) ^ vocab) & 1
    away = ((ids >> 8) & 1) ^ core
    places = turned * (2 * HALF) + away * HALF + (ids >> 10) * 256 + (ids & 255)
    used = lax.broadcasted_iota(jnp.int32, ids.shape, 1) < bag_lengths.T[:, None, :]
    places = jnp.where(used, places, 4 * HALF)
    scores = pl.pallas_call(
        score_kernel,
        out_shape=jax.ShapeDtypeStruct((256,), F32),
        in_specs=[SMEM] + [HBM] + [VMEM] * 2 + [ANY] + [VMEM] * 2,
        out_specs=VMEM,
        scratch_shapes=[
            pltpu.VMEM((4 * HALF + 8, 128), F32),
            pltpu.VMEM((12, 256, 128), F32),
            pltpu.VMEM((1536, 1024), BF),
            pltpu.SemaphoreType.DMA((4,)),
            pltpu.SemaphoreType.DMA((48,)),
        ]
        + [pltpu.SMEM((256,), jnp.int32)] * 48,
        compiler_params=LARGE,
        name="score",
    )(
        part[None],
        places.reshape(-1),
        own,
        other,
        weights,
        b_hidden[None, :],
        w_score[None, :],
    )
    return (table_out.T, accum_out.T, scores)


def solution(mesh):
    shards = ("x", "z")
    every = ("y", "c", "x", "z")
    inner = Mesh(mesh.devices.reshape(8, 2, 4, 8), every)
    return jax.shard_map(
        per_device,
        mesh=inner,
        in_specs=(
            P(shards, None),
            P(shards, None),
            P(every, None),
            P(every),
            P(every),
            P(every, None, None),
            P(every, None),
            P(shards, None),
            P(),
            P(),
        ),
        out_specs=(P(shards, None), P(shards, None), P(every)),
        check_vma=False,
    )
```
